256 devices in a mesh: ctx: 32 (over y_lo, z, core), fsdp: 8 (over y_hi, x).
Axes of the slice: x: 4, y: 4 (y_hi: 2, y_lo: 2; y = y_hi * 2 + y_lo), z: 8, core: 2. Of those that a mesh axis runs over, the one named last changes fastest.
Arguments:
- tokens: bfloat16 [12288, 5120], P('ctx', 'fsdp'), may hold values from -30 to 30
- tangents: bfloat16 [12288, 5120], P('ctx', 'fsdp'), may hold values from -6 to 6
- positions: int32 [12288], P('ctx'), may hold values from 0 to 12287, each once
- frames: int32 [12288], replicated, may hold values from 0 to 7, never falling along the last dimension, each value on 1 to 1560 neighbouring positions
- w_query: bfloat16 [5120, 3072], P('ctx', 'fsdp'), may hold values from -1 to 1
- w_key: bfloat16 [5120, 3072], P('ctx', 'fsdp'), may hold values from -1 to 1
- w_value: bfloat16 [5120, 3072], P('ctx', 'fsdp'), may hold values from -0.078125 to 0.078125
Outputs:
- attended: bfloat16 [12288, 3072], P('ctx', 'fsdp')
- attended_tangent: bfloat16 [12288, 3072], P('ctx', 'fsdp')
The draws below stay inside these ranges and needn't reach their ends.
All inputs are finite; a program needn't handle non-finite values.
Results may differ from the reference program's by a relative error of at most 0.03.
Values may be sent and summed in bfloat16 or wider, within the bound.
A program may use at most 128 MiB of HBM per device.

```python
import math
import jax
import jax.numpy as jnp
import numpy as np
from jax import lax

D = 5120
H = 24
DH = 128
SPAN = 4
FRAME_MOST = 1560
TOK_DEV = 384
TOKENS = 12288
FRAMES = 8


def shared_weight(key):
    values = jax.random.normal(key, (D, H * DH), jnp.float32)
    return jnp.clip(values, -4.0, 4.0) / math.sqrt(D)


def draw_w_query(key, part):
    shared = shared_weight(key)
    return shared.astype(jnp.bfloat16)


def draw_w_key(key, part):
    key = jax.random.fold_in(key, 7)
    own = jnp.clip(jax.random.normal(key, (D, H * DH), jnp.float32), -4.0, 4.0) / math.sqrt(D)
    return own.astype(jnp.bfloat16)


def draw_tokens(key, part):
    key = jax.random.fold_in(key, 11)
    values = jnp.clip(jax.random.normal(key, (TOKENS, D), jnp.float32), -6.0, 6.0)
    return values.astype(jnp.bfloat16)


def steps_of(stream_key, dims, pieces, low, high):
    gain, own = 1.0, jax.random.fold_in(stream_key, 6)
    for position, blocks in pieces:
        steps = jnp.exp(jax.random.uniform(jax.random.fold_in(own, position), (blocks,), jnp.float32, low / len(pieces), high / len(pieces)))
        gain = gain * jnp.repeat(steps, dims[position] // blocks).reshape([-1 if axis == position else 1 for axis in range(len(dims))])
    return gain


def length_profile(amount, total, limit, lean):
    portions = [(1 << 20) // math.isqrt(grade ** lean) + 1 for grade in range(2, amount + 1)]
    rest, counts = total - limit - (amount - 1), [1] * (amount - 1)
    while rest > 0:
        movable = [i for i in range(amount - 1) if counts[i] < limit]
        mass, budget = sum([portions[i] for i in movable]), rest
        for i in movable:
            extra = min(limit - counts[i], max(1, budget * portions[i] // mass), rest)
            counts[i] = counts[i] + extra
            rest = rest - extra
    return np.array([limit] + counts)


def ragged(key, amount, total, limit, skew):
    if amount == 2:
        one = jax.random.randint(key, (), max(1, total - limit), min(limit, total - 1) + 1)
        return jnp.stack([one, total - one])
    sizes = jnp.asarray(length_profile(amount, total, limit, skew), jnp.int32)
    pairs = (amount - 1) // 2
    source_of, sink = sizes[1:1 + 2 * pairs:2], sizes[2:2 + 2 * pairs:2]
    room = jnp.minimum(source_of - 1, limit - sink)
    passed = jax.random.randint(jax.random.fold_in(key, 1), (pairs,), 0, 1 << 20) % (room + 1)
    sizes = sizes.at[1:1 + 2 * pairs:2].set(source_of - passed).at[2:2 + 2 * pairs:2].set(sink + passed)
    return sizes[jax.random.permutation(jax.random.fold_in(key, 2), amount)]


def centred(rng, extent, scale, reach, pieces=(), kind=jnp.bfloat16):
    entries = scale * jax.random.normal(rng, extent, jnp.float32)
    if pieces:
        entries = entries * steps_of(rng, extent, pieces, -0.22, 0.18)
    return jnp.clip(entries, -reach, reach).astype(kind)


def setup_inputs(seed: int = 0) -> dict:
    key_list = jax.random.split(jax.random.key(seed), 8)
    tokens = draw_tokens(jax.random.fold_in(key_list[7], 71), 0)
    tangents = centred(key_list[1], (TOKENS, D), 1.0, 6.0, ((0, 32), (1, 8)))
    positions = jax.random.permutation(key_list[2], TOKENS).astype(jnp.int32)
    frames = jnp.searchsorted(jnp.cumsum(ragged(key_list[3], FRAMES, TOKENS, FRAME_MOST, 0)), jnp.arange(TOKENS), side="right").astype(jnp.int32)
    w_query = draw_w_query(jax.random.fold_in(key_list[7], 71), 0)
    w_key = draw_w_key(jax.random.fold_in(key_list[7], 71), 0)
    w_value = centred(key_list[6], (D, H * DH), D ** -0.5, 0.078125, ((0, 32), (1, 8)))
    return {"tokens": tokens, "tangents": tangents, "positions": positions, "frames": frames, "w_query": w_query, "w_key": w_key, "w_value": w_value}


def one_head(args, allowed):
    query, key, value, query_t, key_t, value_t = args
    scale = DH ** -0.5
    score = jnp.dot(query, key.T, preferred_element_type=jnp.float32) * scale
    score_t = (jnp.dot(query_t, key.T, preferred_element_type=jnp.float32) + jnp.dot(query, key_t.T, preferred_element_type=jnp.float32)) * scale
    score = jnp.where(allowed, score, jnp.float32(-1e30))
    top = jnp.max(score, axis=1, keepdims=True)
    weight = jnp.where(allowed, jnp.exp(score - top), jnp.float32(0.0))
    total = jnp.sum(weight, axis=1, keepdims=True)
    drift = jnp.sum(weight * score_t, axis=1, keepdims=True)
    weight_b = weight.astype(jnp.bfloat16)
    mixed_b = (weight * score_t).astype(jnp.bfloat16)
    plain = jnp.dot(weight_b, value, preferred_element_type=jnp.float32)
    moved = jnp.dot(mixed_b, value, preferred_element_type=jnp.float32) + jnp.dot(weight_b, value_t, preferred_element_type=jnp.float32)
    attended = plain / total
    attended_tangent = moved / total - attended * (drift / total)
    return attended.astype(jnp.bfloat16), attended_tangent.astype(jnp.bfloat16)


def reference(tokens, tangents, positions, frames, w_query, w_key, w_value):
    count = tokens.shape[0]
    blocks = count // TOK_DEV
    rowframe = jnp.take(frames, positions)
    both = jnp.concatenate([tokens, tangents], 0)

    def project(weights):
        made = jnp.dot(both, weights, preferred_element_type=jnp.float32).astype(jnp.bfloat16)
        return made[:count].reshape(blocks, TOK_DEV, H, DH), made[count:].reshape(blocks, TOK_DEV, H, DH)

    query, query_t = project(w_query)
    key, key_t = project(w_key)
    value, value_t = project(w_value)
    frame_blocks = rowframe.reshape(blocks, TOK_DEV)

    def one_block(index):
        picked = ((index - jnp.arange(SPAN + 1, dtype=jnp.int32)) % blocks).astype(jnp.int32)

        def window(array):
            return jnp.take(array, picked, axis=0).reshape((SPAN + 1) * TOK_DEV, H, DH).transpose(1, 0, 2)

        def mine(array):
            return jnp.take(array, index, axis=0).transpose(1, 0, 2)

        key_frames = jnp.take(frame_blocks, picked, axis=0).reshape(-1)
        query_frames = jnp.take(frame_blocks, index, axis=0)
        allowed = key_frames[None, :] <= query_frames[:, None]
        heads = (mine(query), window(key), window(value), mine(query_t), window(key_t), window(value_t))
        return lax.map(lambda args: one_head(args, allowed), heads)

    attended, attended_tangent = lax.map(one_block, jnp.arange(blocks, dtype=jnp.int32))
    attended = attended.transpose(0, 2, 1, 3).reshape(count, H * DH)
    attended_tangent = attended_tangent.transpose(0, 2, 1, 3).reshape(count, H * DH)
    return attended, attended_tangent
```

```python
import functools

import jax
import jax.numpy as jnp
from jax import lax
from jax.experimental import pallas as pl
from jax.experimental.pallas import tpu as pltpu
from jax.sharding import PartitionSpec as P

MESH = pl.DeviceIdType.MESH
DH = 128
HEADS = 3
SPAN = 4
TOK = 384
FEAT = 640
DEPTH = 160
COLS = HEADS * DH
PARTS = (256, 128)
STARTS = (0, 256)
FRAMES = 8
CTX = 32
SCALE = DH**-0.5
LOG2E = 1.4426950408889634
NT = (((1,), (1,)), ((), ()))
N_REMOTE = 90


def kernel(
    pos_ref, frames_ref, tok_ref, tan_ref, wq_ref, wk_ref, wv_ref,
    att_ref, att_t_ref,
    x0, x1, wkv, wq, kv0, kv1, q_all, fr, qf, acc, top, total, drift, pv, mixed,
    local_sem, send_sem, recv_sem,
):
    xs_all, kvs = (x0, x1), (kv0, kv1)
    i, f = lax.axis_index("ctx"), lax.axis_index("fsdp")
    ylo, z, core = i // 16, (i // 2) % 8, i % 2
    yhi, x = f // 4, f % 4

    def at(yl, zz, cc, yh, xx):
        return (yl * 16 + zz * 2 + cc, yh * 4 + xx)

    right, left = at(ylo, z, core, yhi, (x + 1) % 4), at(ylo, z, core, yhi, (x + 3) % 4)
    across = at(ylo, z, core, 1 - yhi, x)
    beside = at(1 - ylo, z, core, yhi, x)
    up, down = at(ylo, (z + 1) % 8, core, yhi, x), at(ylo, (z + 7) % 8, core, yhi, x)
    sibling = at(ylo, z, 1 - core, yhi, x)
    after = ((i + 2) % CTX, f)

    used = []

    def remote(src, dst, device):
        k = len(used)
        copy = pltpu.make_async_remote_copy(
            src, dst, send_sem.at[k], recv_sem.at[k], device_id=device, device_id_type=MESH
        )
        used.append(copy)
        return copy

    def same(ref, device):
        return remote(ref, ref, device)

    def x_at(part, yh, xx, half=None):
        rows = pl.ds(0, 2 * PARTS[part]) if half is None else pl.ds(half * PARTS[part], PARTS[part])
        return xs_all[part].at[yh * 2 + xx // 2, rows, pl.ds(pl.multiple_of((xx % 2) * FEAT, 128), FEAT)]

    def w_at(ref, yl, zz):
        j = yl * 16 + zz * 2 + core
        return ref.at[j // 8, pl.ds(pl.multiple_of((j % 8) * DEPTH, 32), DEPTH)]

    j_pair, j_row = i // 8, pl.ds(pl.multiple_of((i % 8) * DEPTH, 32), DEPTH)
    loads = [
        pltpu.make_async_copy(wk_ref, wkv.at[j_pair, j_row, pl.ds(0, COLS)], local_sem.at[0]),
        pltpu.make_async_copy(wv_ref, wkv.at[j_pair, j_row, pl.ds(COLS, COLS)], local_sem.at[1]),
        pltpu.make_async_copy(wq_ref, wq.at[j_pair, j_row], local_sem.at[2]),
    ]
    for part in range(2):
        rows = pl.ds(STARTS[part], PARTS[part])
        loads.append(pltpu.make_async_copy(tok_ref.at[rows], x_at(part, yhi, x, 0), local_sem.at[3 + 2 * part]))
        loads.append(pltpu.make_async_copy(tan_ref.at[rows], x_at(part, yhi, x, 1), local_sem.at[4 + 2 * part]))
    for k in (0, 1, 3, 4, 2, 5, 6):
        loads[k].start()

    barrier = pltpu.get_barrier_semaphore()
    greeted = [right, left, across, beside, up, down, sibling]
    for d in range(1, SPAN + 1):
        greeted.append(((i + d) % CTX, f))
        greeted.append(((i + CTX - d) % CTX, f))
    for device in greeted:
        pl.semaphore_signal(barrier, inc=1, device_id=device, device_id_type=MESH)
    pl.semaphore_wait(barrier, len(greeted))

    hops = {("own", 1): 4, ("own", -1): 3, ("other", 1): 3, ("other", -1): 4}
    side = {"own": ylo, "other": 1 - ylo}
    ring, kv_sib = {}, []

    def w_share(which, way, step):
        return w_at(wkv, side[which], (z + 8 - way * step) % 8)

    def w_send(which, way, step):
        ring[which, way, step] = same(w_share(which, way, step), up if way == 1 else down)
        ring[which, way, step].start()

    def w_sib(ref):
        kv_sib.append(same(ref, sibling))
        kv_sib[-1].start()

    def w_turn(which, step):
        for way in (1, -1):
            if step < hops[which, way]:
                ring[which, way, step].wait_recv()
                if step + 1 < hops[which, way]:
                    w_send(which, way, step + 1)
                w_sib(w_share(which, way, step + 1))

    loads[0].wait()
    loads[1].wait()
    swap = same(w_at(wkv, ylo, z), beside)
    swap.start()
    w_send("own", 1, 0)
    w_send("own", -1, 0)

    xc = {}

    def x_send(name, part, ref, device):
        xc[name, part] = same(ref, device)
        xc[name, part].start()

    loads[3].wait()
    loads[4].wait()
    x_send("a", 0, x_at(0, yhi, x), right)
    x_send("b", 0, x_at(0, yhi, x), left)
    x_send("c", 0, x_at(0, yhi, x), across)
    w_sib(w_at(wkv, ylo, z))

    position = pos_ref[...]
    row_frame = jnp.zeros_like(position)
    for number in range(1, FRAMES):
        before = jnp.where(frames_ref[...] < number, 1, 0)
        start = jnp.sum(jnp.sum(before, axis=0, keepdims=True), axis=1, keepdims=True)
        row_frame += jnp.where(position >= start, 1, 0)
    fr[0] = jnp.broadcast_to(row_frame, (8, TOK))
    fr_copies = [remote(fr.at[0], fr.at[d], ((i + d) % CTX, f)) for d in range(1, SPAN + 1)]
    for copy in fr_copies:
        copy.start()
    line = lax.broadcasted_iota(jnp.int32, (TOK, TOK), 0)
    column = lax.broadcasted_iota(jnp.int32, (TOK, TOK), 1)
    turned = jnp.sum(
        jnp.where(line == column, row_frame.astype(jnp.float32), 0.0), axis=1, keepdims=True
    )
    qf[...] = jnp.broadcast_to(turned.astype(jnp.int32), (TOK, 128))

    def x_first(part):
        xc["a", part].wait_recv()
        x_send("d", part, x_at(part, yhi, (x + 3) % 4, 0), right)
        xc["b", part].wait_recv()
        x_send("e", part, x_at(part, yhi, (x + 1) % 4, 1), left)

    def x_second(part):
        xc["c", part].wait_recv()
        x_send("f", part, x_at(part, 1 - yhi, x), right)
        x_send("g", part, x_at(part, 1 - yhi, x), left)

    def x_third(part):
        xc["d", part].wait_recv()
        xc["e", part].wait_recv()
        x_send("h", part, x_at(part, yhi, (x + 2) % 4), across)

    def x_last(part):
        for name in ("f", "g", "h"):
            xc[name, part].wait_recv()

    swap.wait_recv()
    w_send("other", 1, 0)
    w_send("other", -1, 0)
    w_sib(w_at(wkv, 1 - ylo, z))
    w_turn("own", 0)
    x_first(0)
    x_second(0)
    w_turn("other", 0)
    loads[5].wait()
    loads[6].wait()
    x_send("c", 1, x_at(1, yhi, x), across)
    w_turn("own", 1)
    x_third(0)
    x_send("a", 1, x_at(1, yhi, x), right)
    x_send("b", 1, x_at(1, yhi, x), left)
    w_turn("other", 1)
    w_turn("own", 2)
    x_second(1)
    w_turn("other", 2)

    q_ring, q_beside, q_sib = [], [], []

    def q_sibling(ref):
        q_sib.append(same(ref, sibling))
        q_sib[-1].start()

    def q_pass(step):
        share = w_at(wq, ylo, (z + step) % 8)
        if step < 7:
            q_ring.append(same(share, down))
            q_ring[-1].start()
        q_beside.append(same(share, beside))
        q_beside[-1].start()
        q_sibling(share)

    def q_turn(step):
        q_ring[step].wait_recv()
        q_pass(step + 1)
        q_beside[step].wait_recv()
        q_sibling(w_at(wq, 1 - ylo, (z + step) % 8))

    loads[2].wait()
    q_pass(0)
    x_first(1)
    w_turn("own", 3)
    w_turn("other", 3)
    x_third(1)
    x_last(0)
    for copy in kv_sib:
        copy.wait_recv()

    def project(part, weights, width, between):
        rows = 2 * PARTS[part]
        for pair in range(4):
            made = jnp.dot(xs_all[part][pair], weights[pair], preferred_element_type=jnp.float32)
            if pair == 0:
                acc[pl.ds(0, rows), pl.ds(0, width)] = made
            else:
                acc[pl.ds(0, rows), pl.ds(0, width)] += made
            between(pair)

    def keep_kv(part):
        rows = PARTS[part]
        for which in range(2):
            for head in range(HEADS):
                columns = pl.ds(which * COLS + head * DH, DH)
                kvs[part][0, which, :, pl.ds(head * 256, DH)] = acc[pl.ds(0, rows), columns].astype(jnp.bfloat16)
                kvs[part][0, which, :, pl.ds(head * 256 + DH, DH)] = acc[pl.ds(rows, rows), columns].astype(
                    jnp.bfloat16
                )

    kva, kvb, siba, sibb = {}, {}, {}, {}

    def kv_start(part):
        kva[part] = remote(kvs[part].at[0], kvs[part].at[2], after)
        kva[part].start()

    def kv_pass(part):
        kva[part].wait_recv()
        kvb[part] = remote(kvs[part].at[2], kvs[part].at[4], after)
        kvb[part].start()
        siba[part] = remote(kvs[part].at[2 * core], kvs[part].at[1], sibling)
        siba[part].start()

    def kv_end(part):
        kvb[part].wait_recv()
        sibb[part] = remote(kvs[part].at[2 + 2 * core], kvs[part].at[3], sibling)
        sibb[part].start()

    project(0, wkv, 2 * COLS, lambda pair: q_turn(pair) if pair < 3 else None)
    keep_kv(0)
    kv_start(0)
    x_last(1)
    project(1, wkv, 2 * COLS, lambda pair: q_turn(3 + pair) if pair < 2 else None)
    keep_kv(1)
    kv_start(1)
    q_turn(5)
    q_turn(6)
    q_beside[7].wait_recv()
    q_sibling(w_at(wq, 1 - ylo, (z + 7) % 8))
    for copy in q_sib:
        copy.wait_recv()
    kv_pass(0)

    for part in range(2):
        project(part, wq, COLS, lambda pair: None)
        rows, at_row = PARTS[part], STARTS[part]
        for head in range(HEADS):
            columns = pl.ds(head * DH, DH)
            q_all[pl.ds(at_row, rows), pl.ds(head * 256 + DH, DH)] = acc[pl.ds(0, rows), columns].astype(jnp.bfloat16)
            q_all[pl.ds(at_row, rows), pl.ds(head * 256, DH)] = acc[pl.ds(rows, rows), columns].astype(jnp.bfloat16)

    def attend(pieces, first):
        def one_head(head, _):
            wide = pl.ds(pl.multiple_of(head * 256, 256), 256)
            slim = pl.ds(pl.multiple_of(head * 256, 256), DH)
            query = q_all[:, pl.ds(pl.multiple_of(head * 256 + DH, DH), DH)]
            both = q_all[:, wide]
            query_frames = qf[:, 0:1]
            scores, scores_t = [], []
            for slot, part in pieces:
                keys = kvs[part].at[slot, 0]
                score = lax.dot_general(query, keys[:, slim], NT, preferred_element_type=jnp.float32)
                score_t = lax.dot_general(both, keys[:, wide], NT, preferred_element_type=jnp.float32)
                key_frames = fr[slot, 0:1, pl.ds(STARTS[part], PARTS[part])]
                scores.append(jnp.where(key_frames <= query_frames, score * (SCALE * LOG2E), -1e30))
                scores_t.append(score_t)
            here = functools.reduce(jnp.maximum, [jnp.max(s, axis=1, keepdims=True) for s in scores])
            if first:
                top_new = here
            else:
                top_old = top[head, :, 0:1]
                top_new = jnp.maximum(top_old, here)
                shrink = jnp.exp2(top_old - top_new)
            lanes, lanes_t = [], []
            out_v, out_m = None, None
            for (slot, part), score, score_t in zip(pieces, scores, scores_t):
                weight = jnp.exp2(score - top_new)
                moved = weight * score_t
                for c in range(0, PARTS[part], 128):
                    lanes.append(weight[:, c : c + 128])
                    lanes_t.append(moved[:, c : c + 128])
                values = kvs[part].at[slot, 1]
                a = jnp.dot(weight.astype(jnp.bfloat16), values[:, wide], preferred_element_type=jnp.float32)
                b = jnp.dot(moved.astype(jnp.bfloat16), values[:, slim], preferred_element_type=jnp.float32)
                out_v = a if out_v is None else out_v + a
                out_m = b if out_m is None else out_m + b
            add = functools.reduce(jnp.add, lanes)
            add_t = functools.reduce(jnp.add, lanes_t)
            top[head] = jnp.broadcast_to(top_new, (TOK, 128))
            if first:
                total[head], drift[head] = add, add_t
                pv[head], mixed[head] = out_v, out_m
            else:
                total[head] = total[head] * shrink + add
                drift[head] = drift[head] * shrink + add_t
                pv[head] = pv[head] * shrink + out_v
                mixed[head] = mixed[head] * shrink + out_m
            return 0

        lax.fori_loop(0, HEADS, one_head, 0)

    attend([(0, 0), (0, 1)], True)
    for copy in fr_copies:
        copy.wait_recv()
    kv_pass(1)
    siba[0].wait_recv()
    attend([(1, 0), (2, 0)], False)
    siba[1].wait_recv()
    attend([(1, 1), (2, 1)], False)
    kv_end(0)
    sibb[0].wait_recv()
    attend([(3, 0), (4, 0)], False)
    kv_end(1)
    sibb[1].wait_recv()
    attend([(3, 1), (4, 1)], False)

    for head in range(HEADS):
        whole = jnp.sum(total[head], axis=1, keepdims=True)
        pull = jnp.sum(drift[head], axis=1, keepdims=True) * SCALE
        attended = pv[head, :, pl.ds(0, DH)] / whole
        moved = mixed[head] * SCALE + pv[head, :, pl.ds(DH, DH)]
        columns = pl.ds(head * DH, DH)
        att_ref[:, columns] = attended.astype(jnp.bfloat16)
        att_t_ref[:, columns] = (moved / whole - attended * (pull / whole)).astype(jnp.bfloat16)

    for copy in used:
        copy.wait_send()


def per_device(tokens, tangents, positions, frames, w_query, w_key, w_value):
    out = jax.ShapeDtypeStruct((TOK, COLS), jnp.bfloat16)
    vmem = pl.BlockSpec(memory_space=pltpu.VMEM)
    anywhere = pl.BlockSpec(memory_space=pl.ANY)
    bf16, f32 = jnp.bfloat16, jnp.float32
    return pl.pallas_call(
        kernel,
        out_shape=(out, out),
        in_specs=[vmem, vmem] + [anywhere] * 5,
        out_specs=(vmem, vmem),
        scratch_shapes=[
            pltpu.VMEM((4, 2 * PARTS[0], 2 * FEAT), bf16),
            pltpu.VMEM((4, 2 * PARTS[1], 2 * FEAT), bf16),
            pltpu.VMEM((4, 8 * DEPTH, 2 * COLS), bf16),
            pltpu.VMEM((4, 8 * DEPTH, COLS), bf16),
            pltpu.VMEM((SPAN + 1, 2, PARTS[0], 2 * COLS), bf16),
            pltpu.VMEM((SPAN + 1, 2, PARTS[1], 2 * COLS), bf16),
            pltpu.VMEM((TOK, 2 * COLS), bf16),
            pltpu.VMEM((SPAN + 1, 8, TOK), jnp.int32),
            pltpu.VMEM((TOK, 128), jnp.int32),
            pltpu.VMEM((2 * PARTS[0], 2 * COLS), f32),
            pltpu.VMEM((HEADS, TOK, 128), f32),
            pltpu.VMEM((HEADS, TOK, 128), f32),
            pltpu.VMEM((HEADS, TOK, 128), f32),
            pltpu.VMEM((HEADS, TOK, 256), f32),
            pltpu.VMEM((HEADS, TOK, 128), f32),
            pltpu.SemaphoreType.DMA((7,)),
            pltpu.SemaphoreType.DMA((N_REMOTE,)),
            pltpu.SemaphoreType.DMA((N_REMOTE,)),
        ],
        compiler_params=pltpu.CompilerParams(
            collective_id=0, has_side_effects=True, vmem_limit_bytes=56 << 20
        ),
        cost_estimate=pl.CostEstimate(flops=12_500_000_000, bytes_accessed=4_000_000, transcendentals=2_300_000),
        name="fused_attention",
    )(
        positions.reshape(1, TOK), frames.reshape(-1, 128), tokens, tangents, w_query, w_key, w_value
    )


def solution(mesh):
    return jax.shard_map(
        per_device,
        mesh=mesh,
        in_specs=(
            P("ctx", "fsdp"),
            P("ctx", "fsdp"),
            P("ctx"),
            P(),
            P("ctx", "fsdp"),
            P("ctx", "fsdp"),
            P("ctx", "fsdp"),
        ),
        out_specs=(P("ctx", "fsdp"), P("ctx", "fsdp")),
        check_vma=False,
    )
```

```python
import functools

import jax
import jax.numpy as jnp
from jax import lax
from jax.experimental import pallas as pl
from jax.experimental.pallas import tpu as pltpu
from jax.sharding import PartitionSpec as P

MESH = pl.DeviceIdType.MESH
DH = 128
HEADS = 3
SPAN = 4
TOK = 384
FEAT = 640
DEPTH = 160
COLS = HEADS * DH
PART = 128
PARTS = TOK // PART
FRAMES = 8
CTX = 32
SCALE = DH**-0.5
LOG2E = 1.4426950408889634
NT = (((1,), (1,)), ((), ()))
N_REMOTE = 105


def kernel(
    pos_ref, frames_ref, tok_ref, tan_ref, wq_ref, wk_ref, wv_ref,
    att_ref, att_t_ref,
    xs, wkv, wq, kv, q_all, fr, qf, acc, top, total, drift, pv, mixed,
    local_sem, send_sem, recv_sem,
):
    i, f = lax.axis_index("ctx"), lax.axis_index("fsdp")
    ylo, z, core = i // 16, (i // 2) % 8, i % 2
    yhi, x = f // 4, f % 4

    def at(yl, zz, cc, yh, xx):
        return (yl * 16 + zz * 2 + cc, yh * 4 + xx)

    right, left = at(ylo, z, core, yhi, (x + 1) % 4), at(ylo, z, core, yhi, (x + 3) % 4)
    across = at(ylo, z, core, 1 - yhi, x)
    beside = at(1 - ylo, z, core, yhi, x)
    up, down = at(ylo, (z + 1) % 8, core, yhi, x), at(ylo, (z + 7) % 8, core, yhi, x)
    sibling = at(ylo, z, 1 - core, yhi, x)
    after = ((i + 2) % CTX, f)

    used = []

    def remote(src, dst, device):
        k = len(used)
        copy = pltpu.make_async_remote_copy(
            src, dst, send_sem.at[k], recv_sem.at[k], device_id=device, device_id_type=MESH
        )
        used.append(copy)
        return copy

    def same(ref, device):
        return remote(ref, ref, device)

    def x_at(part, yh, xx, half=None):
        rows = pl.ds(0, 2 * PART) if half is None else pl.ds(half * PART, PART)
        return xs.at[part, yh * 2 + xx // 2, rows, pl.ds(pl.multiple_of((xx % 2) * FEAT, 128), FEAT)]

    def w_at(ref, yl, zz):
        j = yl * 16 + zz * 2 + core
        return ref.at[j // 8, pl.ds(pl.multiple_of((j % 8) * DEPTH, 32), DEPTH)]

    j_pair, j_row = i // 8, pl.ds(pl.multiple_of((i % 8) * DEPTH, 32), DEPTH)
    loads = [
        pltpu.make_async_copy(wk_ref, wkv.at[j_pair, j_row, pl.ds(0, COLS)], local_sem.at[0]),
        pltpu.make_async_copy(wv_ref, wkv.at[j_pair, j_row, pl.ds(COLS, COLS)], local_sem.at[1]),
        pltpu.make_async_copy(wq_ref, wq.at[j_pair, j_row], local_sem.at[2]),
    ]
    for part in range(PARTS):
        rows = pl.ds(part * PART, PART)
        loads.append(pltpu.make_async_copy(tok_ref.at[rows], x_at(part, yhi, x, 0), local_sem.at[3 + 2 * part]))
        loads.append(pltpu.make_async_copy(tan_ref.at[rows], x_at(part, yhi, x, 1), local_sem.at[4 + 2 * part]))
    for k in (0, 1, 3, 4, 2, 5, 6, 7, 8):
        loads[k].start()

    barrier = pltpu.get_barrier_semaphore()
    greeted = [right, left, across, beside, up, down, sibling]
    for d in range(1, SPAN + 1):
        greeted.append(((i + d) % CTX, f))
        greeted.append(((i + CTX - d) % CTX, f))
    for device in greeted:
        pl.semaphore_signal(barrier, inc=1, device_id=device, device_id_type=MESH)
    pl.semaphore_wait(barrier, len(greeted))

    hops = {("own", 1): 4, ("own", -1): 3, ("other", 1): 3, ("other", -1): 4}
    side = {"own": ylo, "other": 1 - ylo}
    ring, kv_sib = {}, []

    def w_share(which, way, step):
        return w_at(wkv, side[which], (z + 8 - way * step) % 8)

    def w_send(which, way, step):
        ring[which, way, step] = same(w_share(which, way, step), up if way == 1 else down)
        ring[which, way, step].start()

    def w_sib(ref):
        kv_sib.append(same(ref, sibling))
        kv_sib[-1].start()

    def w_turn(which, step):
        for way in (1, -1):
            if step < hops[which, way]:
                ring[which, way, step].wait_recv()
                if step + 1 < hops[which, way]:
                    w_send(which, way, step + 1)
                w_sib(w_share(which, way, step + 1))

    loads[0].wait()
    loads[1].wait()
    swap = same(w_at(wkv, ylo, z), beside)
    swap.start()
    w_send("own", 1, 0)
    w_send("own", -1, 0)

    xc = {}

    def x_send(name, part, ref, device):
        xc[name, part] = same(ref, device)
        xc[name, part].start()

    def x_here(part):
        loads[3 + 2 * part].wait()
        loads[4 + 2 * part].wait()

    def x_own(part):
        x_send("a", part, x_at(part, yhi, x), right)
        x_send("b", part, x_at(part, yhi, x), left)

    def x_swap(part):
        x_send("c", part, x_at(part, yhi, x), across)

    def x_first(part):
        xc["a", part].wait_recv()
        x_send("d", part, x_at(part, yhi, (x + 3) % 4, 0), right)
        xc["b", part].wait_recv()
        x_send("e", part, x_at(part, yhi, (x + 1) % 4, 1), left)
        xc["c", part].wait_recv()
        x_send("f", part, x_at(part, 1 - yhi, x), right)
        x_send("g", part, x_at(part, 1 - yhi, x), left)

    def x_second(part):
        xc["f", part].wait_recv()
        x_send("h", part, x_at(part, 1 - yhi, (x + 3) % 4, 0), right)
        xc["g", part].wait_recv()
        x_send("i", part, x_at(part, 1 - yhi, (x + 1) % 4, 1), left)

    def x_last(part):
        for name in ("d", "e", "h", "i"):
            xc[name, part].wait_recv()

    x_here(0)
    x_own(0)
    x_swap(0)
    w_sib(w_at(wkv, ylo, z))

    position = pos_ref[...]
    row_frame = jnp.zeros_like(position)
    for number in range(1, FRAMES):
        before = jnp.where(frames_ref[...] < number, 1, 0)
        start = jnp.sum(jnp.sum(before, axis=0, keepdims=True), axis=1, keepdims=True)
        row_frame += jnp.where(position >= start, 1, 0)
    fr[0] = jnp.broadcast_to(row_frame, (8, TOK))
    fr_copies = [remote(fr.at[0], fr.at[d], ((i + d) % CTX, f)) for d in range(1, SPAN + 1)]
    for copy in fr_copies:
        copy.start()
    line = lax.broadcasted_iota(jnp.int32, (TOK, TOK), 0)
    column = lax.broadcasted_iota(jnp.int32, (TOK, TOK), 1)
    turned = jnp.sum(
        jnp.where(line == column, row_frame.astype(jnp.float32), 0.0), axis=1, keepdims=True
    )
    qf[...] = jnp.broadcast_to(turned.astype(jnp.int32), (TOK, 128))

    q_ring, q_sib = {}, []

    def q_sibling(ref):
        q_sib.append(same(ref, sibling))
        q_sib[-1].start()

    def q_pass(which, step):
        share = w_at(wq, side[which], (z + step) % 8)
        if step < 7:
            q_ring[which, step] = same(share, down)
            q_ring[which, step].start()
        q_sibling(share)

    def q_turn(step):
        for which in ("own", "other"):
            q_ring[which, step].wait_recv()
            q_pass(which, step + 1)

    swap.wait_recv()
    w_send("other", 1, 0)
    w_send("other", -1, 0)
    w_sib(w_at(wkv, 1 - ylo, z))
    for part in range(1, PARTS):
        x_here(part)
        x_swap(part)
    w_turn("own", 0)
    x_first(0)
    loads[2].wait()
    q_swap = same(w_at(wq, ylo, z), beside)
    q_swap.start()
    w_turn("other", 0)
    w_turn("own", 1)
    x_second(0)
    x_own(1)
    w_turn("other", 1)
    w_turn("own", 2)
    x_first(1)
    w_turn("other", 2)
    q_swap.wait_recv()
    q_pass("own", 0)
    q_pass("other", 0)
    w_turn("own", 3)
    w_turn("other", 3)
    x_last(0)
    for copy in kv_sib:
        copy.wait_recv()

    def project(part, weights, width):
        for pair in range(4):
            made = jnp.dot(xs[part, pair], weights[pair], preferred_element_type=jnp.float32)
            if pair == 0:
                acc[:, pl.ds(0, width)] = made
            else:
                acc[:, pl.ds(0, width)] += made

    def rows_of(part):
        return pl.ds(part * PART, PART)

    def keep_kv(part):
        for which in range(2):
            for head in range(HEADS):
                columns = pl.ds(which * COLS + head * DH, DH)
                kv[0, which, rows_of(part), pl.ds(head * 256, DH)] = acc[pl.ds(0, PART), columns].astype(jnp.bfloat16)
                kv[0, which, rows_of(part), pl.ds(head * 256 + DH, DH)] = acc[pl.ds(PART, PART), columns].astype(
                    jnp.bfloat16
                )

    kva, kvb, siba, sibb = {}, {}, {}, {}

    def kv_at(slot, part):
        return kv.at[slot, :, rows_of(part)]

    def kv_start(part):
        kva[part] = remote(kv_at(0, part), kv_at(2, part), after)
        kva[part].start()

    def kv_pass(part):
        kva[part].wait_recv()
        kvb[part] = remote(kv_at(2, part), kv_at(4, part), after)
        kvb[part].start()
        siba[part] = remote(kv_at(2 * core, part), kv_at(1, part), sibling)
        siba[part].start()

    def kv_end(part):
        kvb[part].wait_recv()
        sibb[part] = remote(kv_at(2 + 2 * core, part), kv_at(3, part), sibling)
        sibb[part].start()

    project(0, wkv, 2 * COLS)
    keep_kv(0)
    kv_start(0)
    x_second(1)
    x_own(2)
    q_turn(0)
    q_turn(1)
    x_last(1)
    project(1, wkv, 2 * COLS)
    keep_kv(1)
    kv_start(1)
    kv_pass(0)
    x_first(2)
    q_turn(2)
    kv_pass(1)
    q_turn(3)
    x_second(2)
    q_turn(4)
    x_last(2)
    project(2, wkv, 2 * COLS)
    keep_kv(2)
    kv_start(2)
    q_turn(5)
    kv_end(0)
    q_turn(6)
    for copy in q_sib:
        copy.wait_recv()
    kv_end(1)

    for part in range(PARTS):
        project(part, wq, COLS)
        for head in range(HEADS):
            columns = pl.ds(head * DH, DH)
            q_all[rows_of(part), pl.ds(head * 256 + DH, DH)] = acc[pl.ds(0, PART), columns].astype(jnp.bfloat16)
            q_all[rows_of(part), pl.ds(head * 256, DH)] = acc[pl.ds(PART, PART), columns].astype(jnp.bfloat16)

    def attend(pieces, first):
        def one_head(head, _):
            wide = pl.ds(pl.multiple_of(head * 256, 256), 256)
            slim = pl.ds(pl.multiple_of(head * 256, 256), DH)
            query = q_all[:, pl.ds(pl.multiple_of(head * 256 + DH, DH), DH)]
            both = q_all[:, wide]
            query_frames = qf[:, 0:1]
            scores, scores_t = [], []
            for slot, start, size in pieces:
                keys = kv.at[slot, 0, pl.ds(start, size)]
                score = lax.dot_general(query, keys[:, slim], NT, preferred_element_type=jnp.float32)
                score_t = lax.dot_general(both, keys[:, wide], NT, preferred_element_type=jnp.float32)
                key_frames = fr[slot, 0:1, pl.ds(start, size)]
                scores.append(jnp.where(key_frames <= query_frames, score * (SCALE * LOG2E), -1e30))
                scores_t.append(score_t)
            here = functools.reduce(jnp.maximum, [jnp.max(s, axis=1, keepdims=True) for s in scores])
            if first:
                top_new = here
            else:
                top_old = top[head, :, 0:1]
                top_new = jnp.maximum(top_old, here)
                shrink = jnp.exp2(top_old - top_new)
            lanes, lanes_t = [], []
            out_v, out_m = None, None
            for (slot, start, size), score, score_t in zip(pieces, scores, scores_t):
                weight = jnp.exp2(score - top_new)
                moved = weight * score_t
                for c in range(0, size, 128):
                    lanes.append(weight[:, c : c + 128])
                    lanes_t.append(moved[:, c : c + 128])
                values = kv.at[slot, 1, pl.ds(start, size)]
                a = jnp.dot(weight.astype(jnp.bfloat16), values[:, wide], preferred_element_type=jnp.float32)
                b = jnp.dot(moved.astype(jnp.bfloat16), values[:, slim], preferred_element_type=jnp.float32)
                out_v = a if out_v is None else out_v + a
                out_m = b if out_m is None else out_m + b
            add = functools.reduce(jnp.add, lanes)
            add_t = functools.reduce(jnp.add, lanes_t)
            top[head] = jnp.broadcast_to(top_new, (TOK, 128))
            if first:
                total[head], drift[head] = add, add_t
                pv[head], mixed[head] = out_v, out_m
            else:
                total[head] = total[head] * shrink + add
                drift[head] = drift[head] * shrink + add_t
                pv[head] = pv[head] * shrink + out_v
                mixed[head] = mixed[head] * shrink + out_m
            return 0

        lax.fori_loop(0, HEADS, one_head, 0)

    early = 2 * PART
    attend([(0, 0, TOK)], True)
    kv_pass(2)
    for copy in fr_copies:
        copy.wait_recv()
    for part in range(2):
        siba[part].wait_recv()
    attend([(1, 0, early), (2, 0, early)], False)
    for part in range(2):
        sibb[part].wait_recv()
    attend([(3, 0, early), (4, 0, early)], False)
    siba[2].wait_recv()
    attend([(1, early, PART), (2, early, PART)], False)
    kv_end(2)
    sibb[2].wait_recv()
    attend([(3, early, PART), (4, early, PART)], False)

    for head in range(HEADS):
        whole = jnp.sum(total[head], axis=1, keepdims=True)
        pull = jnp.sum(drift[head], axis=1, keepdims=True) * SCALE
        attended = pv[head, :, pl.ds(0, DH)] / whole
        moved = mixed[head] * SCALE + pv[head, :, pl.ds(DH, DH)]
        columns = pl.ds(head * DH, DH)
        att_ref[:, columns] = attended.astype(jnp.bfloat16)
        att_t_ref[:, columns] = (moved / whole - attended * (pull / whole)).astype(jnp.bfloat16)

    assert len(used) == N_REMOTE
    for copy in used:
        copy.wait_send()


def per_device(tokens, tangents, positions, frames, w_query, w_key, w_value):
    out = jax.ShapeDtypeStruct((TOK, COLS), jnp.bfloat16)
    vmem = pl.BlockSpec(memory_space=pltpu.VMEM)
    anywhere = pl.BlockSpec(memory_space=pl.ANY)
    bf16, f32 = jnp.bfloat16, jnp.float32
    return pl.pallas_call(
        kernel,
        out_shape=(out, out),
        in_specs=[vmem, vmem] + [anywhere] * 5,
        out_specs=(vmem, vmem),
        scratch_shapes=[
            pltpu.VMEM((PARTS, 4, 2 * PART, 2 * FEAT), bf16),
            pltpu.VMEM((4, 8 * DEPTH, 2 * COLS), bf16),
            pltpu.VMEM((4, 8 * DEPTH, COLS), bf16),
            pltpu.VMEM((SPAN + 1, 2, TOK, 2 * COLS), bf16),
            pltpu.VMEM((TOK, 2 * COLS), bf16),
            pltpu.VMEM((SPAN + 1, 8, TOK), jnp.int32),
            pltpu.VMEM((TOK, 128), jnp.int32),
            pltpu.VMEM((2 * PART, 2 * COLS), f32),
            pltpu.VMEM((HEADS, TOK, 128), f32),
            pltpu.VMEM((HEADS, TOK, 128), f32),
            pltpu.VMEM((HEADS, TOK, 128), f32),
            pltpu.VMEM((HEADS, TOK, 256), f32),
            pltpu.VMEM((HEADS, TOK, 128), f32),
            pltpu.SemaphoreType.DMA((3 + 2 * PARTS,)),
            pltpu.SemaphoreType.DMA((N_REMOTE,)),
            pltpu.SemaphoreType.DMA((N_REMOTE,)),
        ],
        compiler_params=pltpu.CompilerParams(
            collective_id=0, has_side_effects=True, vmem_limit_bytes=56 << 20
        ),
        cost_estimate=pl.CostEstimate(flops=12_500_000_000, bytes_accessed=4_000_000, transcendentals=2_300_000),
        name="fused_attention",
    )(
        positions.reshape(1, TOK), frames.reshape(-1, 128), tokens, tangents, w_query, w_key, w_value
    )


def solution(mesh):
    return jax.shard_map(
        per_device,
        mesh=mesh,
        in_specs=(
            P("ctx", "fsdp"),
            P("ctx", "fsdp"),
            P("ctx"),
            P(),
            P("ctx", "fsdp"),
            P("ctx", "fsdp"),
            P("ctx", "fsdp"),
        ),
        out_specs=(P("ctx", "fsdp"), P("ctx", "fsdp")),
        check_vma=False,
    )
```

```python
import functools

import jax
import jax.numpy as jnp
from jax import lax
from jax.experimental import pallas as pl
from jax.experimental.pallas import tpu as pltpu
from jax.sharding import PartitionSpec as P

MESH = pl.DeviceIdType.MESH
DH = 128
HEADS = 3
SPAN = 4
TOK = 384
FEAT = 640
DEPTH = 160
COLS = HEADS * DH
PART = 128
PARTS = TOK // PART
FRAMES = 8
CTX = 32
SCALE = DH**-0.5
LOG2E = 1.4426950408889634
NT = (((1,), (1,)), ((), ()))
N_REMOTE = 164


def kernel(
    pos_ref, frames_ref, tok_ref, tan_ref, wq_ref, wk_ref, wv_ref,
    att_ref, att_t_ref,
    xs, wkv, wq, kv, q_all, fr, qf, acc, top, total, drift, pv, mixed,
    local_sem, send_sem, recv_sem,
):
    i, f = lax.axis_index("ctx"), lax.axis_index("fsdp")
    ylo, z, core = i // 16, (i // 2) % 8, i % 2
    yhi, x = f // 4, f % 4

    def at(yl, zz, cc, yh, xx):
        return (yl * 16 + zz * 2 + cc, yh * 4 + xx)

    right, left = at(ylo, z, core, yhi, (x + 1) % 4), at(ylo, z, core, yhi, (x + 3) % 4)
    across = at(ylo, z, core, 1 - yhi, x)
    beside = at(1 - ylo, z, core, yhi, x)
    up, down = at(ylo, (z + 1) % 8, core, yhi, x), at(ylo, (z + 7) % 8, core, yhi, x)
    sibling = at(ylo, z, 1 - core, yhi, x)
    after = ((i + 2) % CTX, f)

    used = []

    def remote(src, dst, device):
        k = len(used)
        copy = pltpu.make_async_remote_copy(
            src, dst, send_sem.at[k], recv_sem.at[k], device_id=device, device_id_type=MESH
        )
        used.append(copy)
        return copy

    def same(ref, device):
        return remote(ref, ref, device)

    def x_at(part, yh, xx, half=None):
        rows = pl.ds(0, 2 * PART) if half is None else pl.ds(half * PART, PART)
        return xs.at[part, yh * 2 + xx // 2, rows, pl.ds(pl.multiple_of((xx % 2) * FEAT, 128), FEAT)]

    def w_at(yl, zz, columns=slice(None)):
        j = yl * 16 + zz * 2 + core
        return wkv.at[j // 8, pl.ds(pl.multiple_of((j % 8) * DEPTH, 32), DEPTH), columns]

    j_pair, j_row = i // 8, pl.ds(pl.multiple_of((i % 8) * DEPTH, 32), DEPTH)
    loads = [
        pltpu.make_async_copy(wk_ref, wkv.at[j_pair, j_row, pl.ds(0, COLS)], local_sem.at[0]),
        pltpu.make_async_copy(wv_ref, wkv.at[j_pair, j_row, pl.ds(COLS, COLS)], local_sem.at[1]),
    ]
    for head in range(HEADS):
        loads.append(
            pltpu.make_async_copy(wq_ref.at[:, pl.ds(head * DH, DH)], wq.at[head, i // 2, core], local_sem.at[2 + head])
        )
    for part in range(PARTS):
        rows = pl.ds(part * PART, PART)
        loads.append(pltpu.make_async_copy(tok_ref.at[rows], x_at(part, yhi, x, 0), local_sem.at[5 + 2 * part]))
        loads.append(pltpu.make_async_copy(tan_ref.at[rows], x_at(part, yhi, x, 1), local_sem.at[6 + 2 * part]))
    for k in (0, 1, 5, 6, 2, 3, 4, 7, 8, 9, 10):
        loads[k].start()

    barrier = pltpu.get_barrier_semaphore()
    greeted = [right, left, across, beside, up, down, sibling, after, ((i + CTX - 2) % CTX, f)]
    for device in greeted:
        pl.semaphore_signal(barrier, inc=1, device_id=device, device_id_type=MESH)
    pl.semaphore_wait(barrier, len(greeted))

    hops = {
        ("key", "own", 1): 4, ("key", "own", -1): 3, ("key", "other", 1): 3, ("key", "other", -1): 3,
        ("value", "own", 1): 3, ("value", "own", -1): 4, ("value", "other", 1): 3, ("value", "other", -1): 3,
    }
    side = {"own": ylo, "other": 1 - ylo}
    spans = {"key": pl.ds(0, COLS), "value": pl.ds(COLS, COLS)}
    ring, swap, kv_sib, sent = {}, {}, [], []

    def w_share(kind, which, way, step):
        return w_at(side[which], (z + 8 - way * step) % 8, spans[kind])

    def w_send(kind, which, step):
        for way in (1, -1):
            if step < hops[kind, which, way]:
                ring[kind, which, way, step] = same(w_share(kind, which, way, step), up if way == 1 else down)
                ring[kind, which, way, step].start()

    def w_sib(ref):
        kv_sib.append(same(ref, sibling))
        kv_sib[-1].start()

    def w_turn(kind, which, step):
        for way in (1, -1):
            if step < hops[kind, which, way]:
                ring[kind, which, way, step].wait_recv()
        w_send(kind, which, step + 1)
        for way in (1, -1):
            if step < hops[kind, which, way]:
                w_sib(w_share(kind, which, way, step + 1))

    def w_swap(kind):
        swap[kind] = same(w_at(ylo, z, spans[kind]), beside)
        swap[kind].start()
        w_send(kind, "own", 0)

    def w_far(kind):
        swap[kind, 4] = same(w_at(ylo, (z + 4) % 8, spans[kind]), beside)
        swap[kind, 4].start()

    def w_far_end(kind):
        swap[kind, 4].wait_recv()
        w_sib(w_at(1 - ylo, (z + 4) % 8, spans[kind]))

    def w_swapped(kind):
        swap[kind].wait_recv()
        w_send(kind, "other", 0)
        w_sib(w_at(1 - ylo, z, spans[kind]))

    loads[0].wait()
    loads[1].wait()
    w_swap("key")

    xc = {}

    def x_send(name, part, ref, device):
        xc[name, part] = same(ref, device)
        xc[name, part].start()

    def x_here(part):
        loads[5 + 2 * part].wait()
        loads[6 + 2 * part].wait()

    def x_own(part):
        x_send("a", part, x_at(part, yhi, x), right)
        x_send("b", part, x_at(part, yhi, x), left)

    def x_swap(part):
        x_send("c", part, x_at(part, yhi, x), across)

    def x_first(part):
        xc["a", part].wait_recv()
        x_send("d", part, x_at(part, yhi, (x + 3) % 4, 0), right)
        xc["b", part].wait_recv()
        x_send("e", part, x_at(part, yhi, (x + 1) % 4, 1), left)
        xc["c", part].wait_recv()
        x_send("f", part, x_at(part, 1 - yhi, x), right)
        x_send("g", part, x_at(part, 1 - yhi, x), left)

    def x_second(part):
        xc["f", part].wait_recv()
        x_send("h", part, x_at(part, 1 - yhi, (x + 3) % 4, 0), right)
        xc["g", part].wait_recv()
        x_send("i", part, x_at(part, 1 - yhi, (x + 1) % 4, 1), left)

    def x_last(part):
        for name in ("d", "e", "h", "i"):
            xc[name, part].wait_recv()

    x_here(0)
    x_own(0)
    x_swap(0)
    w_sib(w_at(ylo, z))

    position = pos_ref[...].reshape(1, TOK)
    row_frame = jnp.zeros_like(position)
    for number in range(1, FRAMES):
        before = jnp.where(frames_ref[...] < number, 1, 0)
        start = jnp.sum(jnp.sum(before, axis=0, keepdims=True), axis=1, keepdims=True)
        row_frame += jnp.where(position >= start, 1, 0)
    fr[0] = jnp.broadcast_to(row_frame, (8, TOK))
    fr_copies = [remote(fr.at[0], fr.at[2], after)]
    fr_copies[0].start()

    def fr_pass():
        fr_copies[0].wait_recv()
        fr_copies.append(remote(fr.at[2], fr.at[4], after))
        fr_copies.append(remote(fr.at[2 * core], fr.at[1], sibling))
        fr_copies[1].start()
        fr_copies[2].start()

    def fr_end():
        fr_copies[1].wait_recv()
        fr_copies.append(remote(fr.at[2 + 2 * core], fr.at[3], sibling))
        fr_copies[3].start()
    line = lax.broadcasted_iota(jnp.int32, (TOK, TOK), 0)
    column = lax.broadcasted_iota(jnp.int32, (TOK, TOK), 1)
    turned = jnp.sum(
        jnp.where(line == column, row_frame.astype(jnp.float32), 0.0), axis=1, keepdims=True
    )
    qf[...] = jnp.broadcast_to(turned.astype(jnp.int32), (TOK, 128))

    q_ring, q_swap, q_sib = {}, {}, {}

    def q_share(head, which, step):
        return wq.at[head, side[which] * 8 + (z + step) % 8, core]

    def q_up(head):
        for which in ("own", "other"):
            q_ring[head, which, -1] = same(q_share(head, which, 0), up)
            q_ring[head, which, -1].start()

    def q_pass(head, step):
        for which in ("own", "other"):
            q_ring[head, which, step] = same(q_share(head, which, step), down)
            q_ring[head, which, step].start()

    def q_turn(head, step):
        for which in ("own", "other"):
            q_ring[head, which, step].wait_recv()
        if step < 5:
            q_pass(head, step + 1)
        else:
            for which in ("own", "other"):
                q_ring[head, which, -1].wait_recv()
            q_sib[head] = same(wq.at[head, :, core], sibling)
            q_sib[head].start()

    ring["key", "own", 1, 0].wait_send()
    sent.append(ring["key", "own", 1, 0])
    w_swap("value")
    w_turn("key", "own", 0)
    w_swapped("key")
    w_turn("value", "own", 0)
    w_swapped("value")
    x_here(1)
    x_swap(1)
    x_first(0)
    for head in range(HEADS):
        loads[2 + head].wait()
        q_swap[head] = same(q_share(head, "own", 0), beside)
        q_swap[head].start()
    w_turn("key", "own", 1)
    w_turn("key", "other", 0)
    w_turn("value", "own", 1)
    x_here(2)
    x_swap(2)
    w_turn("value", "other", 0)
    fr_pass()
    x_second(0)
    x_own(1)
    w_turn("key", "own", 2)
    w_turn("key", "other", 1)
    w_turn("value", "own", 2)
    w_turn("value", "other", 1)
    x_first(1)
    w_turn("key", "own", 3)
    w_far("key")
    w_turn("value", "own", 3)
    w_far("value")
    for head in range(HEADS):
        q_swap[head].wait_recv()
        q_up(head)
    q_pass(0, 0)
    w_turn("key", "other", 2)
    q_pass(1, 0)
    w_turn("value", "other", 2)
    fr_end()
    x_last(0)

    def project(part, pairs=range(4), first=True):
        for pair in pairs:
            made = jnp.dot(xs[part, pair], wkv[pair], preferred_element_type=jnp.float32)
            if first:
                acc[...] = made
            else:
                acc[...] += made
            first = False

    def rows_of(part):
        return pl.ds(part * PART, PART)

    kva, kvb, siba, sibb = {}, {}, {}, {}

    def kv_at(slot, which, part):
        return kv.at[slot, which, rows_of(part)]

    def kv_start(part):
        for which in range(2):
            for head in range(HEADS):
                columns = pl.ds(which * COLS + head * DH, DH)
                kv[0, which, rows_of(part), pl.ds(head * 256, DH)] = acc[pl.ds(0, PART), columns].astype(jnp.bfloat16)
                kv[0, which, rows_of(part), pl.ds(head * 256 + DH, DH)] = acc[pl.ds(PART, PART), columns].astype(
                    jnp.bfloat16
                )
            kva[which, part] = remote(kv_at(0, which, part), kv_at(2, which, part), after)
            kva[which, part].start()

    def kv_pass(part):
        for which in range(2):
            kva[which, part].wait_recv()
            kvb[which, part] = remote(kv_at(2, which, part), kv_at(4, which, part), after)
            kvb[which, part].start()
        for which in range(2):
            siba[which, part] = remote(kv_at(2 * core, which, part), kv_at(1, which, part), sibling)
            siba[which, part].start()

    def kv_end(part):
        for which in range(2):
            kvb[which, part].wait_recv()
            sibb[which, part] = remote(kv_at(2 + 2 * core, which, part), kv_at(3, which, part), sibling)
            sibb[which, part].start()

    def arrived(copies, part):
        for which in range(2):
            copies[which, part].wait_recv()

    def ask(head, parts=range(PARTS)):
        for part in parts:
            made = jnp.zeros((2 * PART, DH), jnp.float32)
            for pair in range(4):
                weights = wq[head, pl.ds(pair * 4, 4)].reshape(8 * DEPTH, DH)
                made += jnp.dot(xs[part, pair], weights, preferred_element_type=jnp.float32)
            q_all[rows_of(part), pl.ds(head * 256 + DH, DH)] = made[:PART].astype(jnp.bfloat16)
            q_all[rows_of(part), pl.ds(head * 256, DH)] = made[PART:].astype(jnp.bfloat16)

    def attend(heads, pieces, first=False, last=False):
        def one_head(head, _):
            wide = pl.ds(pl.multiple_of(head * 256, 256), 256)
            slim = pl.ds(pl.multiple_of(head * 256, 256), DH)
            query = q_all[:, pl.ds(pl.multiple_of(head * 256 + DH, DH), DH)]
            both = q_all[:, wide]
            slim_out = pl.ds(pl.multiple_of(head * DH, DH), DH)
            query_frames = qf[:, 0:1]
            scores, scores_t = [], []
            for slot, start, size in pieces:
                keys = kv.at[slot, 0, pl.ds(start, size)]
                score = lax.dot_general(query, keys[:, slim], NT, preferred_element_type=jnp.float32)
                score_t = lax.dot_general(both, keys[:, wide], NT, preferred_element_type=jnp.float32)
                key_frames = fr[slot, 0:1, pl.ds(start, size)]
                scores.append(jnp.where(key_frames <= query_frames, score * (SCALE * LOG2E), -1e30))
                scores_t.append(score_t)
            here = functools.reduce(jnp.maximum, [jnp.max(s, axis=1, keepdims=True) for s in scores])
            if first:
                top_new = here
            else:
                top_old = top[head, :, 0:1]
                top_new = jnp.maximum(top_old, here)
                shrink = jnp.exp2(top_old - top_new)
            lanes, lanes_t = [], []
            out_v, out_m = None, None
            for (slot, start, size), score, score_t in zip(pieces, scores, scores_t):
                weight = jnp.exp2(score - top_new)
                moved = weight * score_t
                for c in range(0, size, 128):
                    lanes.append(weight[:, c : c + 128])
                    lanes_t.append(moved[:, c : c + 128])
                values = kv.at[slot, 1, pl.ds(start, size)]
                a = jnp.dot(weight.astype(jnp.bfloat16), values[:, wide], preferred_element_type=jnp.float32)
                b = jnp.dot(moved.astype(jnp.bfloat16), values[:, slim], preferred_element_type=jnp.float32)
                out_v = a if out_v is None else out_v + a
                out_m = b if out_m is None else out_m + b
            add = functools.reduce(jnp.add, lanes)
            add_t = functools.reduce(jnp.add, lanes_t)
            if last:
                whole = jnp.sum(total[head] * shrink + add, axis=1, keepdims=True)
                pull = jnp.sum(drift[head] * shrink + add_t, axis=1, keepdims=True) * SCALE
                out_v += pv[head] * shrink
                out_m += mixed[head] * shrink
                attended = out_v[:, :DH] / whole
                moved = out_m * SCALE + out_v[:, DH:]
                att_ref[:, slim_out] = attended.astype(jnp.bfloat16)
                att_t_ref[:, slim_out] = (moved / whole - attended * (pull / whole)).astype(jnp.bfloat16)
                return 0
            top[head] = jnp.broadcast_to(top_new, (TOK, 128))
            if first:
                total[head], drift[head] = add, add_t
                pv[head], mixed[head] = out_v, out_m
            else:
                total[head] = total[head] * shrink + add
                drift[head] = drift[head] * shrink + add_t
                pv[head] = pv[head] * shrink + out_v
                mixed[head] = mixed[head] * shrink + out_m
            return 0

        lax.fori_loop(heads[0], heads[-1] + 1, one_head, 0)

    early, every = 2 * PART, range(HEADS)
    mine, near, far = [(0, 0, TOK)], [(1, 0, early), (2, 0, early)], [(3, 0, early), (4, 0, early)]

    for copy in kv_sib:
        copy.wait_recv()
    kv_near = len(kv_sib)
    project(0, (z // 4, 2 + z // 4))
    w_far_end("key")
    w_far_end("value")
    for copy in kv_sib[kv_near:]:
        copy.wait_recv()
    project(0, (1 - z // 4, 3 - z // 4), False)
    kv_start(0)
    q_turn(0, 0)
    x_second(1)
    x_own(2)
    q_turn(0, 1)
    q_turn(1, 0)
    q_pass(2, 0)
    q_turn(0, 2)
    x_last(1)
    project(1)
    kv_start(1)
    q_turn(0, 3)
    q_turn(1, 1)
    q_turn(2, 0)
    x_first(2)
    q_turn(0, 4)
    q_turn(1, 2)
    kv_pass(0)
    q_turn(0, 5)
    q_turn(2, 1)
    q_turn(1, 3)
    q_turn(2, 2)
    q_turn(1, 4)
    x_second(2)
    kv_pass(1)
    q_turn(2, 3)
    q_turn(1, 5)
    q_sib[0].wait_recv()
    ask(0, (0, 1))
    x_last(2)
    project(2)
    kv_start(2)
    ask(0, (2,))
    q_turn(2, 4)
    kv_end(0)
    attend([0], mine, True)
    q_turn(2, 5)
    fr_copies[2].wait_recv()
    fr_copies[3].wait_recv()
    arrived(siba, 0)
    arrived(siba, 1)
    attend([0], near)
    kv_end(1)
    q_sib[1].wait_recv()
    ask(1)
    attend([1], mine, True)
    kv_pass(2)
    attend([1], near)
    q_sib[2].wait_recv()
    ask(2)
    attend([2], mine, True)
    attend([2], near)
    arrived(sibb, 0)
    arrived(sibb, 1)
    attend(every, far)
    arrived(siba, 2)
    attend(every, [(1, early, PART), (2, early, PART)])
    kv_end(2)
    attend(every, [(4, early, PART)])
    arrived(sibb, 2)
    attend(every, [(3, early, PART)], last=True)

    assert len(used) == N_REMOTE
    for copy in used:
        if not any(copy is other for other in sent):
            copy.wait_send()


def per_device(tokens, tangents, positions, frames, w_query, w_key, w_value):
    out = jax.ShapeDtypeStruct((TOK, COLS), jnp.bfloat16)
    vmem = pl.BlockSpec(memory_space=pltpu.VMEM)
    anywhere = pl.BlockSpec(memory_space=pl.ANY)
    bf16, f32 = jnp.bfloat16, jnp.float32
    return pl.pallas_call(
        kernel,
        out_shape=(out, out),
        in_specs=[vmem, vmem] + [anywhere] * 5,
        out_specs=(vmem, vmem),
        scratch_shapes=[
            pltpu.VMEM((PARTS, 4, 2 * PART, 2 * FEAT), bf16),
            pltpu.VMEM((4, 8 * DEPTH, 2 * COLS), bf16),
            pltpu.VMEM((HEADS, CTX // 2, 2, DEPTH, DH), bf16),
            pltpu.VMEM((SPAN + 1, 2, TOK, 2 * COLS), bf16),
            pltpu.VMEM((TOK, 2 * COLS), bf16),
            pltpu.VMEM((SPAN + 1, 8, TOK), jnp.int32),
            pltpu.VMEM((TOK, 128), jnp.int32),
            pltpu.VMEM((2 * PART, 2 * COLS), f32),
            pltpu.VMEM((HEADS, TOK, 128), f32),
            pltpu.VMEM((HEADS, TOK, 128), f32),
            pltpu.VMEM((HEADS, TOK, 128), f32),
            pltpu.VMEM((HEADS, TOK, 256), f32),
            pltpu.VMEM((HEADS, TOK, 128), f32),
            pltpu.SemaphoreType.DMA((2 + HEADS + 2 * PARTS,)),
            pltpu.SemaphoreType.DMA((N_REMOTE,)),
            pltpu.SemaphoreType.DMA((N_REMOTE,)),
        ],
        compiler_params=pltpu.CompilerParams(
            collective_id=0, has_side_effects=True, vmem_limit_bytes=56 << 20
        ),
        cost_estimate=pl.CostEstimate(flops=12_500_000_000, bytes_accessed=4_000_000, transcendentals=2_300_000),
        name="fused_attention",
    )(
        positions, frames.reshape(-1, 128), tokens, tangents, w_query, w_key, w_value
    )


def solution(mesh):
    return jax.shard_map(
        per_device,
        mesh=mesh,
        in_specs=(
            P("ctx", "fsdp"),
            P("ctx", "fsdp"),
            P("ctx"),
            P(),
            P("ctx", "fsdp"),
            P("ctx", "fsdp"),
            P("ctx", "fsdp"),
        ),
        out_specs=(P("ctx", "fsdp"), P("ctx", "fsdp")),
        check_vma=False,
    )
```

```python
import functools

import jax
import jax.numpy as jnp
from jax import lax
from jax.experimental import pallas as pl
from jax.experimental.pallas import tpu as pltpu
from jax.sharding import PartitionSpec as P

MESH = pl.DeviceIdType.MESH
DH = 128
HEADS = 3
SPAN = 4
TOK = 384
FEAT = 640
DEPTH = 160
COLS = HEADS * DH
PART = 128
PARTS = TOK // PART
FRAMES = 8
CTX = 32
SCALE = DH**-0.5
LOG2E = 1.4426950408889634
NT = (((1,), (1,)), ((), ()))
N_REMOTE = 164


def kernel(
    pos_ref, frames_ref, tok_ref, tan_ref, wq_ref, wk_ref, wv_ref,
    att_ref, att_t_ref,
    xs, wkv, wq, kv, q_all, fr, qf, acc, top, total, drift, pv, mixed,
    local_sem, send_sem, recv_sem,
):
    i, f = lax.axis_index("ctx"), lax.axis_index("fsdp")
    ylo, z, core = i // 16, (i // 2) % 8, i % 2
    yhi, x = f // 4, f % 4

    def at(yl, zz, cc, yh, xx):
        return (yl * 16 + zz * 2 + cc, yh * 4 + xx)

    right, left = at(ylo, z, core, yhi, (x + 1) % 4), at(ylo, z, core, yhi, (x + 3) % 4)
    across = at(ylo, z, core, 1 - yhi, x)
    beside = at(1 - ylo, z, core, yhi, x)
    up, down = at(ylo, (z + 1) % 8, core, yhi, x), at(ylo, (z + 7) % 8, core, yhi, x)
    sibling = at(ylo, z, 1 - core, yhi, x)
    after = ((i + 2) % CTX, f)

    used = []

    def remote(src, dst, device):
        k = len(used)
        copy = pltpu.make_async_remote_copy(
            src, dst, send_sem.at[k], recv_sem.at[k], device_id=device, device_id_type=MESH
        )
        used.append(copy)
        return copy

    def same(ref, device):
        return remote(ref, ref, device)

    def x_at(part, yh, xx, half=None):
        rows = pl.ds(0, 2 * PART) if half is None else pl.ds(half * PART, PART)
        return xs.at[part, yh * 2 + xx // 2, rows, pl.ds(pl.multiple_of((xx % 2) * FEAT, 128), FEAT)]

    def w_at(yl, zz, columns=slice(None)):
        j = yl * 16 + zz * 2 + core
        return wkv.at[j // 8, pl.ds(pl.multiple_of((j % 8) * DEPTH, 32), DEPTH), columns]

    j_pair, j_row = i // 8, pl.ds(pl.multiple_of((i % 8) * DEPTH, 32), DEPTH)
    loads = [
        pltpu.make_async_copy(wk_ref, wkv.at[j_pair, j_row, pl.ds(0, COLS)], local_sem.at[0]),
        pltpu.make_async_copy(wv_ref, wkv.at[j_pair, j_row, pl.ds(COLS, COLS)], local_sem.at[1]),
    ]
    for head in range(HEADS):
        loads.append(
            pltpu.make_async_copy(wq_ref.at[:, pl.ds(head * DH, DH)], wq.at[head, i // 2, core], local_sem.at[2 + head])
        )
    for part in range(PARTS):
        rows = pl.ds(part * PART, PART)
        loads.append(pltpu.make_async_copy(tok_ref.at[rows], x_at(part, yhi, x, 0), local_sem.at[5 + 2 * part]))
        loads.append(pltpu.make_async_copy(tan_ref.at[rows], x_at(part, yhi, x, 1), local_sem.at[6 + 2 * part]))
    for k in (0, 1, 5, 6, 2, 3, 4, 7, 8, 9, 10):
        loads[k].start()

    barrier = pltpu.get_barrier_semaphore()
    greeted = [right, left, across, beside, up, down, sibling, after, ((i + CTX - 2) % CTX, f)]
    for device in greeted:
        pl.semaphore_signal(barrier, inc=1, device_id=device, device_id_type=MESH)
    pl.semaphore_wait(barrier, len(greeted))

    hops = {
        ("key", "own", 1): 4, ("key", "own", -1): 3, ("key", "other", 1): 3, ("key", "other", -1): 3,
        ("value", "own", 1): 3, ("value", "own", -1): 4, ("value", "other", 1): 3, ("value", "other", -1): 3,
    }
    side = {"own": ylo, "other": 1 - ylo}
    spans = {"key": pl.ds(0, COLS), "value": pl.ds(COLS, COLS)}
    ring, swap, kv_sib, sent = {}, {}, [], []

    def w_share(kind, which, way, step):
        return w_at(side[which], (z + 8 - way * step) % 8, spans[kind])

    def w_send(kind, which, step):
        for way in (1, -1):
            if step < hops[kind, which, way]:
                ring[kind, which, way, step] = same(w_share(kind, which, way, step), up if way == 1 else down)
                ring[kind, which, way, step].start()

    def w_sib(ref):
        kv_sib.append(same(ref, sibling))
        kv_sib[-1].start()

    def w_turn(kind, which, step):
        for way in (1, -1):
            if step < hops[kind, which, way]:
                ring[kind, which, way, step].wait_recv()
        w_send(kind, which, step + 1)
        for way in (1, -1):
            if step < hops[kind, which, way]:
                w_sib(w_share(kind, which, way, step + 1))

    def w_swap(kind):
        swap[kind] = same(w_at(ylo, z, spans[kind]), beside)
        swap[kind].start()
        w_send(kind, "own", 0)

    def w_far(kind):
        swap[kind, 4] = same(w_at(ylo, (z + 4) % 8, spans[kind]), beside)
        swap[kind, 4].start()

    def w_far_end(kind):
        swap[kind, 4].wait_recv()
        w_sib(w_at(1 - ylo, (z + 4) % 8, spans[kind]))

    def w_swapped(kind):
        swap[kind].wait_recv()
        w_send(kind, "other", 0)
        w_sib(w_at(1 - ylo, z, spans[kind]))

    loads[0].wait()
    loads[1].wait()
    w_swap("key")

    xc = {}

    def x_send(name, part, ref, device):
        xc[name, part] = same(ref, device)
        xc[name, part].start()

    def x_here(part):
        loads[5 + 2 * part].wait()
        loads[6 + 2 * part].wait()

    def x_own(part):
        x_send("a", part, x_at(part, yhi, x), right)
        x_send("b", part, x_at(part, yhi, x), left)

    def x_swap(part):
        x_send("c", part, x_at(part, yhi, x), across)

    def x_first(part):
        xc["a", part].wait_recv()
        x_send("d", part, x_at(part, yhi, (x + 3) % 4, 0), right)
        xc["b", part].wait_recv()
        x_send("e", part, x_at(part, yhi, (x + 1) % 4, 1), left)
        xc["c", part].wait_recv()
        x_send("f", part, x_at(part, 1 - yhi, x), right)
        x_send("g", part, x_at(part, 1 - yhi, x), left)

    def x_second(part):
        xc["f", part].wait_recv()
        x_send("h", part, x_at(part, 1 - yhi, (x + 3) % 4, 0), right)
        xc["g", part].wait_recv()
        x_send("i", part, x_at(part, 1 - yhi, (x + 1) % 4, 1), left)

    def x_last(part):
        for name in ("d", "e", "h", "i"):
            xc[name, part].wait_recv()

    x_here(0)
    x_own(0)
    x_swap(0)
    w_sib(w_at(ylo, z))

    position = pos_ref[...].reshape(1, TOK)
    row_frame = jnp.zeros_like(position)
    for number in range(1, FRAMES):
        before = jnp.where(frames_ref[...] < number, 1, 0)
        start = jnp.sum(jnp.sum(before, axis=0, keepdims=True), axis=1, keepdims=True)
        row_frame += jnp.where(position >= start, 1, 0)
    fr[0] = jnp.broadcast_to(row_frame, (8, TOK))
    fr_copies = [remote(fr.at[0], fr.at[2], after)]
    fr_copies[0].start()

    def fr_pass():
        fr_copies[0].wait_recv()
        fr_copies.append(remote(fr.at[2], fr.at[4], after))
        fr_copies.append(remote(fr.at[2 * core], fr.at[1], sibling))
        fr_copies[1].start()
        fr_copies[2].start()

    def fr_end():
        fr_copies[1].wait_recv()
        fr_copies.append(remote(fr.at[2 + 2 * core], fr.at[3], sibling))
        fr_copies[3].start()
    line = lax.broadcasted_iota(jnp.int32, (TOK, TOK), 0)
    column = lax.broadcasted_iota(jnp.int32, (TOK, TOK), 1)
    turned = jnp.sum(
        jnp.where(line == column, row_frame.astype(jnp.float32), 0.0), axis=1, keepdims=True
    )
    qf[...] = jnp.broadcast_to(turned.astype(jnp.int32), (TOK, 128))

    q_ring, q_swap, q_sib = {}, {}, {}

    def q_share(head, which, step):
        return wq.at[head, side[which] * 8 + (z + step) % 8, core]

    def q_up(head):
        for which in ("own", "other"):
            q_ring[head, which, -1] = same(q_share(head, which, 0), up)
            q_ring[head, which, -1].start()

    def q_pass(head, step):
        for which in ("own", "other"):
            q_ring[head, which, step] = same(q_share(head, which, step), down)
            q_ring[head, which, step].start()

    def q_turn(head, step):
        for which in ("own", "other"):
            q_ring[head, which, step].wait_recv()
        if step < 5:
            q_pass(head, step + 1)
        else:
            for which in ("own", "other"):
                q_ring[head, which, -1].wait_recv()
            q_sib[head] = same(wq.at[head, :, core], sibling)
            q_sib[head].start()

    ring["key", "own", 1, 0].wait_send()
    sent.append(ring["key", "own", 1, 0])
    w_swap("value")
    w_turn("key", "own", 0)
    w_swapped("key")
    w_turn("value", "own", 0)
    w_swapped("value")
    x_first(0)
    x_here(1)
    x_swap(1)
    for head in range(HEADS):
        loads[2 + head].wait()
        q_swap[head] = same(q_share(head, "own", 0), beside)
        q_swap[head].start()
    w_turn("key", "own", 1)
    w_turn("key", "other", 0)
    w_turn("value", "own", 1)
    x_here(2)
    x_swap(2)
    w_turn("value", "other", 0)
    fr_pass()
    x_second(0)
    x_own(1)
    w_turn("key", "own", 2)
    w_turn("key", "other", 1)
    w_turn("value", "own", 2)
    w_turn("value", "other", 1)
    x_first(1)
    w_turn("key", "own", 3)
    w_far("key")
    w_turn("value", "own", 3)
    w_far("value")
    for head in range(HEADS):
        q_swap[head].wait_recv()
        q_up(head)
    q_pass(0, 0)
    w_turn("key", "other", 2)
    q_pass(1, 0)
    w_turn("value", "other", 2)
    fr_end()
    x_last(0)

    def project(part, pairs=range(4), first=True):
        for pair in pairs:
            made = jnp.dot(xs[part, pair], wkv[pair], preferred_element_type=jnp.float32)
            if first:
                acc[...] = made
            else:
                acc[...] += made
            first = False

    def rows_of(part):
        return pl.ds(part * PART, PART)

    kva, kvb, siba, sibb = {}, {}, {}, {}

    def kv_at(slot, which, part):
        return kv.at[slot, which, rows_of(part)]

    def kv_start(part):
        for which in range(2):
            for head in range(HEADS):
                columns = pl.ds(which * COLS + head * DH, DH)
                kv[0, which, rows_of(part), pl.ds(head * 256, DH)] = acc[pl.ds(0, PART), columns].astype(jnp.bfloat16)
                kv[0, which, rows_of(part), pl.ds(head * 256 + DH, DH)] = acc[pl.ds(PART, PART), columns].astype(
                    jnp.bfloat16
                )
            kva[which, part] = remote(kv_at(0, which, part), kv_at(2, which, part), after)
            kva[which, part].start()

    def kv_pass(part):
        for which in range(2):
            kva[which, part].wait_recv()
            kvb[which, part] = remote(kv_at(2, which, part), kv_at(4, which, part), after)
            kvb[which, part].start()
        for which in range(2):
            siba[which, part] = remote(kv_at(2 * core, which, part), kv_at(1, which, part), sibling)
            siba[which, part].start()

    def kv_end(part):
        for which in range(2):
            kvb[which, part].wait_recv()
            sibb[which, part] = remote(kv_at(2 + 2 * core, which, part), kv_at(3, which, part), sibling)
            sibb[which, part].start()

    def arrived(copies, part):
        for which in range(2):
            copies[which, part].wait_recv()

    def ask(head, parts=range(PARTS)):
        for part in parts:
            made = jnp.zeros((2 * PART, DH), jnp.float32)
            for pair in range(4):
                weights = wq[head, pl.ds(pair * 4, 4)].reshape(8 * DEPTH, DH)
                made += jnp.dot(xs[part, pair], weights, preferred_element_type=jnp.float32)
            q_all[rows_of(part), pl.ds(head * 256 + DH, DH)] = made[:PART].astype(jnp.bfloat16)
            q_all[rows_of(part), pl.ds(head * 256, DH)] = made[PART:].astype(jnp.bfloat16)

    def attend(heads, pieces, first=False, last=False):
        def one_head(head, _):
            wide = pl.ds(pl.multiple_of(head * 256, 256), 256)
            slim = pl.ds(pl.multiple_of(head * 256, 256), DH)
            query = q_all[:, pl.ds(pl.multiple_of(head * 256 + DH, DH), DH)]
            both = q_all[:, wide]
            slim_out = pl.ds(pl.multiple_of(head * DH, DH), DH)
            query_frames = qf[:, 0:1]
            scores, scores_t = [], []
            for slot, start, size in pieces:
                keys = kv.at[slot, 0, pl.ds(start, size)]
                score = lax.dot_general(query, keys[:, slim], NT, preferred_element_type=jnp.float32)
                score_t = lax.dot_general(both, keys[:, wide], NT, preferred_element_type=jnp.float32)
                key_frames = fr[slot, 0:1, pl.ds(start, size)]
                scores.append(jnp.where(key_frames <= query_frames, score * (SCALE * LOG2E), -1e30))
                scores_t.append(score_t)
            here = functools.reduce(jnp.maximum, [jnp.max(s, axis=1, keepdims=True) for s in scores])
            if first:
                top_new = here
            else:
                top_old = top[head, :, 0:1]
                top_new = jnp.maximum(top_old, here)
                shrink = jnp.exp2(top_old - top_new)
            lanes, lanes_t = [], []
            out_v, out_m = None, None
            for (slot, start, size), score, score_t in zip(pieces, scores, scores_t):
                weight = jnp.exp2(score - top_new)
                moved = weight * score_t
                for c in range(0, size, 128):
                    lanes.append(weight[:, c : c + 128])
                    lanes_t.append(moved[:, c : c + 128])
                values = kv.at[slot, 1, pl.ds(start, size)]
                a = jnp.dot(weight.astype(jnp.bfloat16), values[:, wide], preferred_element_type=jnp.float32)
                b = jnp.dot(moved.astype(jnp.bfloat16), values[:, slim], preferred_element_type=jnp.float32)
                out_v = a if out_v is None else out_v + a
                out_m = b if out_m is None else out_m + b
            add = functools.reduce(jnp.add, lanes)
            add_t = functools.reduce(jnp.add, lanes_t)
            if last:
                whole = jnp.sum(total[head] * shrink + add, axis=1, keepdims=True)
                pull = jnp.sum(drift[head] * shrink + add_t, axis=1, keepdims=True) * SCALE
                out_v += pv[head] * shrink
                out_m += mixed[head] * shrink
                attended = out_v[:, :DH] / whole
                moved = out_m * SCALE + out_v[:, DH:]
                att_ref[:, slim_out] = attended.astype(jnp.bfloat16)
                att_t_ref[:, slim_out] = (moved / whole - attended * (pull / whole)).astype(jnp.bfloat16)
                return 0
            top[head] = jnp.broadcast_to(top_new, (TOK, 128))
            if first:
                total[head], drift[head] = add, add_t
                pv[head], mixed[head] = out_v, out_m
            else:
                total[head] = total[head] * shrink + add
                drift[head] = drift[head] * shrink + add_t
                pv[head] = pv[head] * shrink + out_v
                mixed[head] = mixed[head] * shrink + out_m
            return 0

        lax.fori_loop(heads[0], heads[-1] + 1, one_head, 0)

    early, every = 2 * PART, range(HEADS)
    mine, near, far = [(0, 0, TOK)], [(1, 0, early), (2, 0, early)], [(3, 0, early), (4, 0, early)]

    for copy in kv_sib:
        copy.wait_recv()
    kv_near = len(kv_sib)
    project(0, (z // 4, 2 + z // 4))
    w_far_end("key")
    w_far_end("value")
    for copy in kv_sib[kv_near:]:
        copy.wait_recv()
    project(0, (1 - z // 4, 3 - z // 4), False)
    kv_start(0)
    q_turn(0, 0)
    x_second(1)
    x_own(2)
    q_turn(0, 1)
    q_turn(1, 0)
    q_pass(2, 0)
    q_turn(0, 2)
    x_last(1)
    project(1)
    kv_start(1)
    q_turn(0, 3)
    q_turn(1, 1)
    q_turn(2, 0)
    x_first(2)
    q_turn(0, 4)
    q_turn(1, 2)
    kv_pass(0)
    q_turn(0, 5)
    q_turn(2, 1)
    q_turn(1, 3)
    q_turn(2, 2)
    q_turn(1, 4)
    x_second(2)
    kv_pass(1)
    q_turn(2, 3)
    q_turn(1, 5)
    q_sib[0].wait_recv()
    ask(0, (0, 1))
    x_last(2)
    project(2)
    kv_start(2)
    ask(0, (2,))
    q_turn(2, 4)
    kv_end(0)
    attend([0], mine, True)
    q_turn(2, 5)
    fr_copies[2].wait_recv()
    fr_copies[3].wait_recv()
    arrived(siba, 0)
    arrived(siba, 1)
    attend([0], near)
    kv_end(1)
    q_sib[1].wait_recv()
    ask(1)
    attend([1], mine, True)
    kv_pass(2)
    attend([1], near)
    q_sib[2].wait_recv()
    ask(2)
    attend([2], mine, True)
    attend([2], near)
    arrived(sibb, 0)
    arrived(sibb, 1)
    attend(every, far)
    arrived(siba, 2)
    attend(every, [(1, early, PART), (2, early, PART)])
    kv_end(2)
    attend(every, [(4, early, PART)])
    arrived(sibb, 2)
    attend(every, [(3, early, PART)], last=True)

    assert len(used) == N_REMOTE
    for copy in used:
        if not any(copy is other for other in sent):
            copy.wait_send()


def per_device(tokens, tangents, positions, frames, w_query, w_key, w_value):
    out = jax.ShapeDtypeStruct((TOK, COLS), jnp.bfloat16)
    vmem = pl.BlockSpec(memory_space=pltpu.VMEM)
    anywhere = pl.BlockSpec(memory_space=pl.ANY)
    bf16, f32 = jnp.bfloat16, jnp.float32
    return pl.pallas_call(
        kernel,
        out_shape=(out, out),
        in_specs=[vmem, vmem] + [anywhere] * 5,
        out_specs=(vmem, vmem),
        scratch_shapes=[
            pltpu.VMEM((PARTS, 4, 2 * PART, 2 * FEAT), bf16),
            pltpu.VMEM((4, 8 * DEPTH, 2 * COLS), bf16),
            pltpu.VMEM((HEADS, CTX // 2, 2, DEPTH, DH), bf16),
            pltpu.VMEM((SPAN + 1, 2, TOK, 2 * COLS), bf16),
            pltpu.VMEM((TOK, 2 * COLS), bf16),
            pltpu.VMEM((SPAN + 1, 8, TOK), jnp.int32),
            pltpu.VMEM((TOK, 128), jnp.int32),
            pltpu.VMEM((2 * PART, 2 * COLS), f32),
            pltpu.VMEM((HEADS, TOK, 128), f32),
            pltpu.VMEM((HEADS, TOK, 128), f32),
            pltpu.VMEM((HEADS, TOK, 128), f32),
            pltpu.VMEM((HEADS, TOK, 256), f32),
            pltpu.VMEM((HEADS, TOK, 128), f32),
            pltpu.SemaphoreType.DMA((2 + HEADS + 2 * PARTS,)),
            pltpu.SemaphoreType.DMA((N_REMOTE,)),
            pltpu.SemaphoreType.DMA((N_REMOTE,)),
        ],
        compiler_params=pltpu.CompilerParams(
            collective_id=0, has_side_effects=True, vmem_limit_bytes=56 << 20
        ),
        cost_estimate=pl.CostEstimate(flops=12_500_000_000, bytes_accessed=4_000_000, transcendentals=2_300_000),
        name="fused_attention",
    )(
        positions, frames.reshape(-1, 128), tokens, tangents, w_query, w_key, w_value
    )


def solution(mesh):
    return jax.shard_map(
        per_device,
        mesh=mesh,
        in_specs=(
            P("ctx", "fsdp"),
            P("ctx", "fsdp"),
            P("ctx"),
            P(),
            P("ctx", "fsdp"),
            P("ctx", "fsdp"),
            P("ctx", "fsdp"),
        ),
        out_specs=(P("ctx", "fsdp"), P("ctx", "fsdp")),
        check_vma=False,
    )
```
